32 devices in a mesh: groups: 2 (over x), box: 16 (over z, y, core).
Axes of the slice: x: 2, y: 2, z: 4, core: 2. Of those that a mesh axis runs over, the one named last changes fastest.
Arguments:
- coeffs: bfloat16 [4, 64, 65536], P(None, None, ('groups', 'box')), parts along dimension 2, may hold values from -6 to 6
- operators: bfloat16 [4, 8, 64, 128], replicated, may hold values from -0.5 to 0.5
- pattern: int32 [4, 65536], P(None, 'groups'), parts along dimension 1, may hold values from 0 to 7
- owner_order: int32 [65536], P(('groups', 'box')), parts along dimension 0, may hold values from 0 to 2047, as said below
Outputs:
- targets: bfloat16 [4, 64, 65536], P(None, None, ('groups', 'box')), parts along dimension 2
The draws below stay inside these ranges and needn't reach their ends.
There are 2 independent parts, one for each index of `groups`. The reference program is written for one: setup_inputs(seed, part) draws one part's arguments, and reference() takes and returns one part's arrays. A program takes and returns all parts, laid end to end along the dimension named above; an argument that names none is the same for every part. Nothing has to cross between parts.
Inputs may be any that keep to these rules, and one draw needn't show every extreme that they name: `owner_order`: each aligned block of 2048 entries is a permutation of 0 .. 2047.
All inputs are finite; a program needn't handle non-finite values.
Results may differ from the reference program's by a relative error of at most 0.0066.
Values may be sent and summed in bfloat16 or wider, within the bound.
No kernel may reach another device: no remote copies, remote signals or barrier semaphores. Data moves between devices by JAX's collectives and lax.ppermute only.
A program may use at most 64 MiB of HBM per device.

```python
import jax
import jax.numpy as jnp

RANK = 64
RHS = 4
LEVELS = 4
TABLES = 8
BOX_DEV = 2048
BOXES = 32768
N_BOX = 16


def draw_owner_order(key, part):
    key = jax.random.fold_in(key, 7)
    scores = jax.random.randint(key, (N_BOX, BOX_DEV), 0, 65536)
    scores = scores * BOX_DEV + jnp.arange(BOX_DEV, dtype=jnp.int32)[None, :]
    order = jnp.argsort(scores, axis=1, stable=True).astype(jnp.int32)
    return order.reshape(N_BOX * BOX_DEV)


def place_ends(entries, key, low, high):
    spot = [jax.random.randint(jax.random.fold_in(key, axis), (), 0, length) for axis, length in enumerate(entries.shape)]
    longest = entries.shape.index(max(entries.shape))
    neighbour = spot[:longest] + [(spot[longest] + 1) % entries.shape[longest]] + spot[longest + 1:]
    return entries.at[tuple(spot)].set(low).at[tuple(neighbour)].set(high)


def level_of(own_key, extent, shards, smallest, high):
    loudness, own = 1.0, jax.random.fold_in(own_key, 6)
    for dim, shards_of in shards:
        heights = jnp.exp(jax.random.uniform(jax.random.fold_in(own, dim), (shards_of,), jnp.float32, smallest / len(shards), high / len(shards)))
        loudness = loudness * jnp.repeat(heights, extent[dim] // shards_of).reshape([-1 if axis == dim else 1 for axis in range(len(extent))])
    return loudness


def centred(rng, dims, deviation, most, cuts=(), kind=jnp.bfloat16):
    level = level_of(rng, dims, cuts, -0.22, 0.18) if cuts else 1.0
    array = jax.random.normal(rng, dims, jnp.float32) * deviation * level
    return jnp.minimum(jnp.maximum(array, -most), most).astype(kind)


def setup_inputs(seed: int = 0, part: int = 0) -> dict:
    arg_keys = jax.random.split(jax.random.key(seed), 5)
    part_keys = jax.random.split(jax.random.fold_in(arg_keys[4], part), 5)
    coeffs = centred(part_keys[0], (RHS, RANK, BOXES), 1.0, 6.0, ((2, 16),))
    operators = centred(arg_keys[1], (LEVELS, TABLES, RANK, 2 * RANK), (2 * RANK) ** -0.5, 0.5)
    pattern = place_ends(jax.random.randint(part_keys[2], (LEVELS, BOXES), 0, TABLES), jax.random.fold_in(part_keys[2], 1), 0, TABLES - 1).astype(jnp.int32)
    owner_order = draw_owner_order(jax.random.fold_in(jax.random.fold_in(arg_keys[4], part), 71), part)
    return {"coeffs": coeffs, "operators": operators, "pattern": pattern, "owner_order": owner_order}


def reference(coeffs, operators, pattern, owner_order):
    bit_count = N_BOX.bit_length() - 1
    total = coeffs.shape[2]
    state = coeffs
    for level_index in range(LEVELS):
        stride = BOX_DEV * (2 ** (bit_count - 1 - level_index))
        shaped = state.reshape(RHS, RANK, total // (2 * stride), 2, stride)
        first_half = shaped[:, :, :, 0, :]
        second_half = shaped[:, :, :, 1, :]
        joined = jnp.concatenate([first_half, second_half], axis=1).astype(jnp.float32)
        chosen = pattern[level_index].reshape(total // (2 * stride), 2, stride)
        first_pick = chosen[:, 0, :][None, None]
        second_pick = chosen[:, 1, :][None, None]
        first_new = jnp.zeros(first_half.shape, jnp.float32)
        second_new = jnp.zeros(second_half.shape, jnp.float32)
        for table_index in range(TABLES):
            matrix = operators[level_index, table_index].astype(jnp.float32)
            product = jnp.einsum("oi,sibk->sobk", matrix, joined)
            first_new = first_new + jnp.where(first_pick == table_index, product, 0.0)
            second_new = second_new + jnp.where(second_pick == table_index, product, 0.0)
        state = jnp.stack([first_new, second_new], axis=3).reshape(RHS, RANK, total).astype(jnp.bfloat16)
    piece = BOX_DEV // N_BOX
    relaid = state.reshape(RHS, RANK, N_BOX, N_BOX, piece).transpose(0, 1, 3, 2, 4).reshape(RHS, RANK, N_BOX, BOX_DEV)
    index_table = owner_order.reshape(N_BOX, BOX_DEV)[None, None]
    result = jnp.take_along_axis(relaid, index_table, axis=3)
    return result.reshape(RHS, RANK, total)
```

```python
import jax
import jax.numpy as jnp
from jax import lax
from jax.experimental import pallas as pl
from jax.experimental.pallas import tpu as pltpu
from jax.sharding import PartitionSpec as P

LANES = 128


def levels_kernel(received, tables, picks, order, out, state):
    tiles, rhs, rank, _ = received.shape
    level_count, rows, _ = tables.shape
    table_count = rows // rank
    groups = rank // 8
    boxes = tiles * LANES
    source = lax.broadcasted_iota(jnp.int32, (boxes, 512), 0)

    for level in range(level_count):
        apart = tiles >> (level + 1)
        before = received if level == 0 else state
        for low in range(tiles):
            if low & apart:
                continue
            pair = (low, low + apart)
            joined = jnp.concatenate(
                [jnp.concatenate([before[tile, r] for tile in pair], axis=0) for r in range(rhs)], axis=1
            )
            product = jnp.dot(tables[level], joined, preferred_element_type=jnp.float32)
            product = product.reshape(table_count, groups, 8, rhs * LANES)
            for tile in pair:
                pick = jnp.broadcast_to(picks[level, tile : tile + 1, :], (8, LANES))
                pick = jnp.concatenate([pick] * rhs, axis=1)
                choices = [product[t] for t in range(table_count)]
                bit = 1
                while len(choices) > 1:
                    odd = (pick & bit) != 0
                    choices = [jnp.where(odd, high, low_) for low_, high in zip(choices[::2], choices[1::2])]
                    bit *= 2
                chosen = choices[0].reshape(rank, rhs * LANES).astype(jnp.bfloat16)
                for r in range(rhs):
                    state[tile, r] = chosen[:, r * LANES : (r + 1) * LANES]

    flat = jnp.concatenate([state[tile].reshape(rhs * rank, LANES) for tile in range(tiles)], axis=1)
    for start in range(0, boxes, 512):
        wanted = order[:, start : start + 512]
        hot = jnp.where(source == wanted, 1.0, 0.0).astype(jnp.bfloat16)
        placed = jnp.dot(flat, hot, preferred_element_type=jnp.float32).astype(jnp.bfloat16)
        out[:, :, start : start + 512] = placed.reshape(rhs, rank, 512)


def run_levels(received, tables, picks, order):
    tiles, rhs, rank, _ = received.shape
    return pl.pallas_call(
        levels_kernel,
        out_shape=jax.ShapeDtypeStruct((rhs, rank, tiles * LANES), jnp.bfloat16),
        in_specs=[pl.BlockSpec(memory_space=pltpu.VMEM)] * 4,
        out_specs=pl.BlockSpec(memory_space=pltpu.VMEM),
        scratch_shapes=[pltpu.VMEM((tiles, rhs, rank, LANES), jnp.bfloat16)],
        compiler_params=pltpu.CompilerParams(vmem_limit_bytes=40 * 2**20),
        cost_estimate=pl.CostEstimate(flops=4 * 10**9, bytes_accessed=4 * 2**20, transcendentals=0),
    )(received, tables, picks, order)


def body(coeffs, operators, pattern, owner_order):
    device_count = lax.axis_size("box")
    device_index = lax.axis_index("box")
    rhs, rank, boxes = coeffs.shape
    level_count, table_count = operators.shape[:2]
    piece = boxes // device_count
    tiles = boxes // LANES

    sent = coeffs.reshape(rhs, rank, device_count, piece).transpose(2, 0, 1, 3)
    received = lax.all_to_all(sent, "box", split_axis=0, concat_axis=0, tiled=True)
    received = received.reshape(tiles, device_count // tiles, rhs, rank, piece)
    received = received.transpose(0, 2, 3, 1, 4).reshape(tiles, rhs, rank, LANES)

    picks = pattern.reshape(level_count, device_count, device_count, piece)
    picks = lax.dynamic_index_in_dim(picks, device_index, 2, keepdims=False)
    picks = picks.reshape(level_count, tiles, LANES)
    tables = operators.reshape(level_count, table_count * rank, 2 * rank)
    return run_levels(received, tables, picks, owner_order.reshape(1, boxes))


def solution(mesh):
    return jax.shard_map(
        body,
        mesh=mesh,
        in_specs=(P(None, None, ("groups", "box")), P(), P(None, "groups"), P(("groups", "box"))),
        out_specs=P(None, None, ("groups", "box")),
        check_vma=False,
    )
```

```python
import functools

import jax
import jax.numpy as jnp
from jax import lax
from jax.experimental import pallas as pl
from jax.experimental.pallas import tpu as pltpu
from jax.sharding import PartitionSpec as P

LANES = 128
STRIP = 512
LATE = 1
NEAR = 4
PACK_VMEM = 56 * 2**20
VMEM = pl.BlockSpec(memory_space=pltpu.VMEM)
SMEM = pl.BlockSpec(memory_space=pltpu.SMEM)


import functools

import jax
import jax.numpy as jnp
from jax import lax
from jax.experimental import pallas as pl
from jax.experimental.pallas import tpu as pltpu
from jax.sharding import PartitionSpec as P

LANES = 128
EARLY = 2
PACK_VMEM = 56 * 2**20
NEAR = 4
VMEM = pl.BlockSpec(memory_space=pltpu.VMEM)
SMEM = pl.BlockSpec(memory_space=pltpu.SMEM)


def pack_kernel(me, coeffs, most, *refs):
    near, sem = refs[:-1], refs[-1]
    devices, first = most.shape[:2]
    rhs = coeffs.shape[0]
    copies = []
    for j in range(devices):
        copies.append((coeffs.at[0:first, :, j * LANES : (j + 1) * LANES], most.at[j]))
    for d, ref in enumerate(near):
        for s in range(ref.shape[0]):
            tile = me[0] ^ (s * NEAR + d)
            lanes = pl.ds(pl.multiple_of(tile * LANES, LANES), LANES)
            copies.append((coeffs.at[first:rhs, :, lanes], ref.at[s]))
    copies = [pltpu.make_async_copy(a, b, sem.at[n]) for n, (a, b) in enumerate(copies)]
    for copy in copies:
        copy.start()
    for copy in copies:
        copy.wait()


def pack(me, coeffs, late):
    rhs, rank, boxes = coeffs.shape
    devices = boxes // LANES
    shapes = [(devices, rhs - late, rank, LANES)] + [(devices // NEAR, late, rank, LANES)] * NEAR
    return pl.pallas_call(
        pack_kernel,
        out_shape=[jax.ShapeDtypeStruct(s, coeffs.dtype) for s in shapes],
        in_specs=[SMEM, pl.BlockSpec(memory_space=pl.ANY)],
        out_specs=[VMEM] * len(shapes),
        scratch_shapes=[pltpu.SemaphoreType.DMA((2 * devices,))],
        compiler_params=pltpu.CompilerParams(vmem_limit_bytes=PACK_VMEM),
    )(me, coeffs)


def regroup_kernel(*refs):
    count = refs[-1].shape[0]
    before, after = refs[:count], refs[count:]
    for j, ref in enumerate(after):
        for i in range(count):
            ref[i] = before[i][j]


def regroup(before):
    count = before[0].shape[0]
    shape = (len(before), *before[0].shape[1:])
    return pl.pallas_call(
        regroup_kernel,
        out_shape=[jax.ShapeDtypeStruct(shape, before[0].dtype)] * count,
        in_specs=[VMEM] * len(before),
        out_specs=[VMEM] * count,
        compiler_params=pltpu.CompilerParams(vmem_limit_bytes=8 * 2**20),
    )(*before)


def all_levels(source, tables, picks, state, rhs):
    tiles, _, rank, _ = state.shape
    level_count, rows, _ = tables.shape
    table_count = rows // rank
    for level in range(level_count):
        apart = tiles >> (level + 1)
        before = source if level == 0 else lambda tile, r: state[tile, r]
        for low in range(tiles):
            if low & apart:
                continue
            pair = (low, low + apart)
            joined = jnp.concatenate(
                [jnp.concatenate([before(tile, r) for tile in pair], axis=0) for r in range(rhs)], axis=1
            )
            product = jnp.dot(tables[level], joined, preferred_element_type=jnp.float32)
            product = product.reshape(table_count, rank // 8, 8, rhs * LANES)
            for tile in pair:
                pick = jnp.broadcast_to(picks[level, tile : tile + 1, :], (8, LANES))
                pick = jnp.concatenate([pick] * rhs, axis=1)
                choices = [product[t] for t in range(table_count)]
                bit = 1
                while len(choices) > 1:
                    odd = (pick & bit) != 0
                    choices = [jnp.where(odd, b, a) for a, b in zip(choices[::2], choices[1::2])]
                    bit *= 2
                chosen = choices[0].reshape(rank, rhs * LANES).astype(jnp.bfloat16)
                for r in range(rhs):
                    state[tile, r] = chosen[:, r * LANES : (r + 1) * LANES]


def lay_out(states, order, out, placed, sem):
    rows = []
    for state in states:
        tiles, rhs, rank, _ = state.shape
        rows.append(jnp.concatenate([state[tile].reshape(rhs * rank, LANES) for tile in range(tiles)], axis=1))
    flat = jnp.concatenate(rows, axis=0)
    source = lax.broadcasted_iota(jnp.int32, (out.shape[2], STRIP), 0)
    copies = []
    for number, start in enumerate(range(0, out.shape[2], STRIP)):
        columns = slice(start, start + STRIP)
        hot = jnp.where(source == order[:, columns], 1.0, 0.0).astype(jnp.bfloat16)
        strip = jnp.dot(flat, hot, preferred_element_type=jnp.float32)
        placed[:, :, columns] = strip.astype(jnp.bfloat16).reshape(out.shape[0], rank, STRIP)
        copies.append(pltpu.make_async_copy(placed.at[:, :, columns], out.at[:, :, columns], sem.at[number]))
        copies[-1].start()
    for copy in copies:
        copy.wait()


def first_kernel(received, tables, picks, state):
    all_levels(lambda tile, r: received[tile, r], tables, picks, state, received.shape[1])


def run_first(received, tables, picks):
    rhs = received.shape[1]
    return pl.pallas_call(
        first_kernel,
        out_shape=jax.ShapeDtypeStruct(received.shape, jnp.bfloat16),
        in_specs=[VMEM] * 3,
        out_specs=VMEM,
        compiler_params=pltpu.CompilerParams(vmem_limit_bytes=16 * 2**20),
        cost_estimate=pl.CostEstimate(flops=rhs * 10**9, bytes_accessed=rhs * 2**20, transcendentals=0),
    )(received, tables, picks)


def last_kernel(me, tables, picks, order, done, *refs):
    far, (out, state, placed, sem) = refs[:-4], refs[-4:]
    states = [done]
    if far:
        for s, ref in enumerate(far):
            for d in range(NEAR):
                state[me[0] ^ (s * NEAR + d)] = ref[d]
        all_levels(lambda tile, r: state[tile, r], tables, picks, state, state.shape[1])
        states.append(state)
    lay_out(states, order, out, placed, sem)


def run_last(me, tables, picks, order, done, far):
    tiles, first, rank, _ = done.shape
    boxes, late = tiles * LANES, far[0].shape[1] if far else 0
    return pl.pallas_call(
        last_kernel,
        out_shape=jax.ShapeDtypeStruct((first + late, rank, boxes), jnp.bfloat16),
        in_specs=[SMEM] + [VMEM] * (4 + len(far)),
        out_specs=pl.BlockSpec(memory_space=pl.ANY),
        scratch_shapes=[
            pltpu.VMEM((tiles, max(late, 1), rank, LANES), jnp.bfloat16),
            pltpu.VMEM((first + late, rank, boxes), jnp.bfloat16),
            pltpu.SemaphoreType.DMA((boxes // STRIP,)),
        ],
        compiler_params=pltpu.CompilerParams(vmem_limit_bytes=40 * 2**20),
        cost_estimate=pl.CostEstimate(flops=5 * 10**9, bytes_accessed=2 * 2**20, transcendentals=0),
    )(me, tables, picks, order, done, *far)


def across(block, distance):
    count = lax.axis_size("box")
    return lax.ppermute(block, "box", [(i, i ^ distance) for i in range(count)])


def body(coeffs, operators, pattern, owner_order):
    device_count = lax.axis_size("box")
    device_index = lax.axis_index("box")
    rhs, rank, boxes = coeffs.shape
    level_count, table_count = operators.shape[:2]
    piece = boxes // device_count
    tiles = boxes // LANES
    picks = pattern.reshape(level_count, device_count, device_count, piece)
    picks = lax.dynamic_index_in_dim(picks, device_index, 2, keepdims=False)
    picks = picks.reshape(level_count, tiles, LANES)
    tables = operators.reshape(level_count, table_count * rank, 2 * rank)
    me = device_index.reshape(1).astype(jnp.int32)
    order = owner_order.reshape(1, boxes)

    if piece != LANES:
        sent = coeffs.reshape(rhs, rank, device_count, piece).transpose(2, 0, 1, 3)
        received = lax.all_to_all(sent, "box", split_axis=0, concat_axis=0, tiled=True)
        received = received.reshape(tiles, device_count // tiles, rhs, rank, piece)
        received = received.transpose(0, 2, 3, 1, 4).reshape(tiles, rhs, rank, LANES)
        return run_last(me, tables, picks, order, run_first(received, tables, picks), [])

    most, *near = pack(me, coeffs, LATE)
    received = lax.all_to_all(most, "box", split_axis=0, concat_axis=0, tiled=True)
    near = [near[0]] + [across(near[d], d) for d in range(1, NEAR)]
    far = regroup(near)
    far = [far[0]] + [across(far[s], s * NEAR) for s in range(1, len(far))]
    done = run_first(received, tables, picks)
    return run_last(me, tables, picks, order, done, far)


def solution(mesh):
    return jax.shard_map(
        body,
        mesh=mesh,
        in_specs=(P(None, None, ("groups", "box")), P(), P(None, "groups"), P(("groups", "box"))),
        out_specs=P(None, None, ("groups", "box")),
        check_vma=False,
    )
```

```python
import functools

import jax
import jax.numpy as jnp
from jax import lax
from jax.experimental import pallas as pl
from jax.experimental.pallas import tpu as pltpu
from jax.sharding import PartitionSpec as P

LANES = 128
STRIP = 512
EARLY = 2
NEAR = 4
PACK_VMEM = 52 * 2**20
EARLY_COST = 16
FIRST_COST = 2
FIRST_VMEM = 24 * 2**20
LAST_VMEM = 24 * 2**20
VMEM = pl.BlockSpec(memory_space=pltpu.VMEM)
SMEM = pl.BlockSpec(memory_space=pltpu.SMEM)


import functools

import jax
import jax.numpy as jnp
from jax import lax
from jax.experimental import pallas as pl
from jax.experimental.pallas import tpu as pltpu
from jax.sharding import PartitionSpec as P

LANES = 128
EARLY = 2
PACK_VMEM = 52 * 2**20
FIRST_COST = 2
NEAR = 4
VMEM = pl.BlockSpec(memory_space=pltpu.VMEM)
SMEM = pl.BlockSpec(memory_space=pltpu.SMEM)


def pack_kernel(early, me, coeffs, operators, pattern, tables, picks, *refs):
    refs, sem = refs[:-1], refs[-1]
    near, far = refs[:NEAR], refs[NEAR:]
    rhs, _, boxes = coeffs.shape
    copies = [(operators, tables)]
    for tile in range(picks.shape[0]):
        lanes = pl.ds(pl.multiple_of(tile * boxes + me[0] * LANES, LANES), LANES)
        copies.append((pattern.at[:, lanes], picks.at[tile]))
    for s in range(len(far)):
        for d in range(NEAR):
            tile = me[0] ^ (s * NEAR + d)
            lanes = pl.ds(pl.multiple_of(tile * LANES, LANES), LANES)
            copies.append((coeffs.at[0:early, :, lanes], far[s].at[d]))
            tile = s * NEAR + ((me[0] % NEAR) ^ d)
            lanes = pl.ds(pl.multiple_of(tile * LANES, LANES), LANES)
            copies.append((coeffs.at[early:rhs, :, lanes], near[d].at[s]))
    copies = [pltpu.make_async_copy(a, b, sem.at[n]) for n, (a, b) in enumerate(copies)]
    for copy in copies:
        copy.start()
    for copy in copies:
        copy.wait()


def pack(me, coeffs, operators, pattern, early):
    rhs, rank, boxes = coeffs.shape
    tiles = boxes // LANES
    planes = tiles // NEAR
    shapes = [(planes, rhs - early, rank, LANES)] * NEAR + [(NEAR, early, rank, LANES)] * planes
    packed = pl.pallas_call(
        functools.partial(pack_kernel, early),
        out_shape=[
            jax.ShapeDtypeStruct(operators.shape, operators.dtype),
            jax.ShapeDtypeStruct((tiles, pattern.shape[0], LANES), pattern.dtype),
        ]
        + [jax.ShapeDtypeStruct(s, coeffs.dtype) for s in shapes],
        in_specs=[SMEM] + [pl.BlockSpec(memory_space=pl.ANY)] * 3,
        out_specs=[VMEM] * (2 + len(shapes)),
        scratch_shapes=[pltpu.SemaphoreType.DMA((1 + 3 * tiles,))],
        compiler_params=pltpu.CompilerParams(vmem_limit_bytes=PACK_VMEM),
    )(me, coeffs, operators, pattern)
    return packed[:2], packed[2 : 2 + NEAR], packed[2 + NEAR :]


def late_kernel(*refs):
    near, late = refs[:-1], refs[-1]
    for d, ref in enumerate(near):
        for z in range(late.shape[0]):
            late[z, d] = ref[z]


def late_blocks(near):
    planes = near[0].shape[0]
    return pl.pallas_call(
        late_kernel,
        out_shape=jax.ShapeDtypeStruct((planes, len(near), *near[0].shape[1:]), near[0].dtype),
        in_specs=[VMEM] * len(near),
        out_specs=VMEM,
        compiler_params=pltpu.CompilerParams(vmem_limit_bytes=8 * 2**20),
    )(*near)


def early_kernel(*refs):
    far, early = refs[:-NEAR], refs[-NEAR:]
    for s, ref in enumerate(far):
        for d in range(NEAR):
            early[d][s] = ref[d]


def early_blocks(far):
    return pl.pallas_call(
        early_kernel,
        out_shape=[jax.ShapeDtypeStruct((len(far), *far[0].shape[1:]), far[0].dtype)] * NEAR,
        in_specs=[VMEM] * len(far),
        out_specs=[VMEM] * NEAR,
        compiler_params=pltpu.CompilerParams(vmem_limit_bytes=8 * 2**20),
        cost_estimate=pl.CostEstimate(flops=EARLY_COST * 10**9, bytes_accessed=2**10, transcendentals=0),
    )(*far)


def all_levels(source, tables, picks, state, rhs):
    tiles, _, rank, _ = state.shape
    level_count, rows, _ = tables.shape
    table_count = rows // rank
    for level in range(level_count):
        apart = tiles >> (level + 1)
        before = source if level == 0 else lambda tile, r: state[tile, r]
        for low in range(tiles):
            if low & apart:
                continue
            pair = (low, low + apart)
            joined = jnp.concatenate(
                [jnp.concatenate([before(tile, r) for tile in pair], axis=0) for r in range(rhs)], axis=1
            )
            product = jnp.dot(tables[level], joined, preferred_element_type=jnp.float32)
            product = product.reshape(table_count, rank // 8, 8, rhs * LANES)
            for tile in pair:
                pick = jnp.broadcast_to(picks[tile, level : level + 1, :], (8, LANES))
                pick = jnp.concatenate([pick] * rhs, axis=1)
                choices = [product[t] for t in range(table_count)]
                bit = 1
                while len(choices) > 1:
                    odd = (pick & bit) != 0
                    choices = [jnp.where(odd, b, a) for a, b in zip(choices[::2], choices[1::2])]
                    bit *= 2
                chosen = choices[0].reshape(rank, rhs * LANES).astype(jnp.bfloat16)
                for r in range(rhs):
                    state[tile, r] = chosen[:, r * LANES : (r + 1) * LANES]


def flat_rows(state):
    tiles, rhs, rank, _ = state.shape
    return jnp.concatenate([state[tile].reshape(rhs * rank, LANES) for tile in range(tiles)], axis=1)


def ones_at(order, start):
    source = lax.broadcasted_iota(jnp.int32, (order.shape[1], STRIP), 0)
    return jnp.where(source == order[:, start : start + STRIP], 1.0, 0.0).astype(jnp.bfloat16)


def put(flat, hot, placed, start):
    strip = jnp.dot(flat, hot, preferred_element_type=jnp.float32).astype(jnp.bfloat16)
    placed[:, :, start : start + STRIP] = strip.reshape(*placed.shape[:2], STRIP)


def whole_kernel(received, tables, picks, order, out, state):
    all_levels(lambda tile, r: received[tile, r], tables, picks, state, received.shape[1])
    flat = flat_rows(state)
    for start in range(0, out.shape[2], STRIP):
        put(flat, ones_at(order, start), out, start)


def run_whole(received, tables, picks, order):
    tiles, rhs, rank, _ = received.shape
    return pl.pallas_call(
        whole_kernel,
        out_shape=jax.ShapeDtypeStruct((rhs, rank, tiles * LANES), jnp.bfloat16),
        in_specs=[VMEM] * 4,
        out_specs=VMEM,
        scratch_shapes=[pltpu.VMEM(received.shape, jnp.bfloat16)],
        compiler_params=pltpu.CompilerParams(vmem_limit_bytes=40 * 2**20),
    )(received, tables, picks, order)


def first_kernel(me, tables, picks, *refs):
    near, state = refs[:-1], refs[-1]
    for d, ref in enumerate(near):
        for s in range(ref.shape[0]):
            state[me[0] ^ (s * NEAR + d)] = ref[s]
    all_levels(lambda tile, r: state[tile, r], tables, picks, state, state.shape[1])


def run_first(me, tables, picks, near):
    planes, rhs, rank, _ = near[0].shape
    return pl.pallas_call(
        first_kernel,
        out_shape=jax.ShapeDtypeStruct((planes * len(near), rhs, rank, LANES), jnp.bfloat16),
        in_specs=[SMEM] + [VMEM] * (2 + len(near)),
        out_specs=VMEM,
        compiler_params=pltpu.CompilerParams(vmem_limit_bytes=FIRST_VMEM),
        cost_estimate=pl.CostEstimate(flops=FIRST_COST * 10**9, bytes_accessed=2**10, transcendentals=0),
    )(me, tables, picks, *near)


def last_kernel(me, tables, picks, order, done, late, out, state, placed, sem):
    for z in range(late.shape[0]):
        for d in range(NEAR):
            state[z * NEAR + ((me[0] % NEAR) ^ d)] = late[z, d]
    all_levels(lambda tile, r: state[tile, r], tables, picks, state, state.shape[1])
    flat = jnp.concatenate([flat_rows(done), flat_rows(state)], axis=0)
    copies = []
    for start in range(0, out.shape[2], STRIP):
        columns = slice(start, start + STRIP)
        put(flat, ones_at(order, start), placed, start)
        copies.append(pltpu.make_async_copy(placed.at[:, :, columns], out.at[:, :, columns], sem.at[start // STRIP]))
        copies[-1].start()
    for copy in copies:
        copy.wait()


def run_last(me, tables, picks, order, done, late):
    tiles, early, rank, _ = done.shape
    boxes, more = tiles * LANES, late.shape[2]
    return pl.pallas_call(
        last_kernel,
        out_shape=jax.ShapeDtypeStruct((early + more, rank, boxes), jnp.bfloat16),
        in_specs=[SMEM] + [VMEM] * 5,
        out_specs=pl.BlockSpec(memory_space=pl.ANY),
        scratch_shapes=[
            pltpu.VMEM((tiles, more, rank, LANES), jnp.bfloat16),
            pltpu.VMEM((early + more, rank, boxes), jnp.bfloat16),
            pltpu.SemaphoreType.DMA((boxes // STRIP,)),
        ],
        compiler_params=pltpu.CompilerParams(vmem_limit_bytes=LAST_VMEM),
        cost_estimate=pl.CostEstimate(flops=5 * 10**9, bytes_accessed=2 * 2**20, transcendentals=0),
    )(me, tables, picks, order, done, late)


def across(block, distance):
    count = lax.axis_size("box")
    return lax.ppermute(block, "box", [(i, i ^ distance) for i in range(count)])


def body(coeffs, operators, pattern, owner_order):
    device_count = lax.axis_size("box")
    device_index = lax.axis_index("box")
    rhs, rank, boxes = coeffs.shape
    level_count, table_count = operators.shape[:2]
    piece = boxes // device_count
    tiles = boxes // LANES
    me = device_index.reshape(1).astype(jnp.int32)
    order = owner_order.reshape(1, boxes)
    tables = operators.reshape(level_count, table_count * rank, 2 * rank)

    if piece != LANES:
        picks = pattern.reshape(level_count, device_count, device_count, piece)
        picks = lax.dynamic_index_in_dim(picks, device_index, 2, keepdims=False)
        picks = picks.reshape(level_count, tiles, LANES).transpose(1, 0, 2)
        sent = coeffs.reshape(rhs, rank, device_count, piece).transpose(2, 0, 1, 3)
        received = lax.all_to_all(sent, "box", split_axis=0, concat_axis=0, tiled=True)
        received = received.reshape(tiles, device_count // tiles, rhs, rank, piece)
        received = received.transpose(0, 2, 3, 1, 4).reshape(tiles, rhs, rank, LANES)
        return run_whole(received, tables, picks, order)

    (tables, picks), near, far = pack(me, coeffs, tables, pattern, EARLY)
    far = [far[0]] + [across(far[s], s * NEAR) for s in range(1, len(far))]
    near = [near[0]] + [across(near[d], d) for d in range(1, NEAR)]
    columns = [[z * NEAR + d for z in range(len(far))] for d in range(NEAR)]
    late = lax.all_to_all(late_blocks(near), "box", 0, 0, tiled=True, axis_index_groups=columns)
    early = early_blocks(far)
    early = [early[0]] + [across(early[d], d) for d in range(1, NEAR)]
    done = run_first(me, tables, picks, early)
    return run_last(me, tables, picks, order, done, late)


def solution(mesh):
    return jax.shard_map(
        body,
        mesh=mesh,
        in_specs=(P(None, None, ("groups", "box")), P(), P(None, "groups"), P(("groups", "box"))),
        out_specs=P(None, None, ("groups", "box")),
        check_vma=False,
    )
```

```python
import functools

import jax
import jax.numpy as jnp
from jax import lax
from jax.experimental import pallas as pl
from jax.experimental.pallas import tpu as pltpu
from jax.sharding import PartitionSpec as P

LANES = 128
STRIP = 512
EARLY = 2
NEAR = 4
PACK_VMEM = 52 * 2**20
EARLY_COST = 16
FIRST_COST = 2
FIRST_VMEM = 24 * 2**20
LAST_VMEM = 24 * 2**20
VMEM = pl.BlockSpec(memory_space=pltpu.VMEM)
SMEM = pl.BlockSpec(memory_space=pltpu.SMEM)


def in_turn(count):
    return [0] + list(range(max(count // 2, 1), count)) + list(range(1, count // 2))


def pack_kernel(early, me, coeffs, operators, pattern, tables, picks, *refs):
    refs, sem = refs[:-1], refs[-1]
    near, far = refs[:NEAR], refs[NEAR:]
    rhs, _, boxes = coeffs.shape
    copies = [(operators, tables)]
    for tile in range(picks.shape[0]):
        lanes = pl.ds(pl.multiple_of(tile * boxes + me[0] * LANES, LANES), LANES)
        copies.append((pattern.at[:, lanes], picks.at[tile]))
    for s in range(len(far)):
        for d in range(NEAR):
            tile = me[0] ^ (s * NEAR + d)
            lanes = pl.ds(pl.multiple_of(tile * LANES, LANES), LANES)
            copies.append((coeffs.at[0:early, :, lanes], far[s].at[d]))
            tile = s * NEAR + ((me[0] % NEAR) ^ d)
            lanes = pl.ds(pl.multiple_of(tile * LANES, LANES), LANES)
            copies.append((coeffs.at[early:rhs, :, lanes], near[d].at[s]))
    copies = [pltpu.make_async_copy(a, b, sem.at[n]) for n, (a, b) in enumerate(copies)]
    for copy in copies:
        copy.start()
    for copy in copies:
        copy.wait()


def pack(me, coeffs, operators, pattern, early):
    rhs, rank, boxes = coeffs.shape
    tiles = boxes // LANES
    planes = tiles // NEAR
    shapes = [(planes, rhs - early, rank, LANES)] * NEAR + [(NEAR, early, rank, LANES)] * planes
    packed = pl.pallas_call(
        functools.partial(pack_kernel, early),
        out_shape=[
            jax.ShapeDtypeStruct(operators.shape, operators.dtype),
            jax.ShapeDtypeStruct((tiles, pattern.shape[0], LANES), pattern.dtype),
        ]
        + [jax.ShapeDtypeStruct(s, coeffs.dtype) for s in shapes],
        in_specs=[SMEM] + [pl.BlockSpec(memory_space=pl.ANY)] * 3,
        out_specs=[VMEM] * (2 + len(shapes)),
        scratch_shapes=[pltpu.SemaphoreType.DMA((1 + 3 * tiles,))],
        compiler_params=pltpu.CompilerParams(vmem_limit_bytes=PACK_VMEM),
    )(me, coeffs, operators, pattern)
    return packed[:2], packed[2 : 2 + NEAR], packed[2 + NEAR :]


def late_kernel(*refs):
    near, late = refs[:-1], refs[-1]
    for d, ref in zip(in_turn(NEAR), near):
        for z in range(late.shape[0]):
            late[z, d] = ref[z]


def late_blocks(near):
    planes = near[0].shape[0]
    return pl.pallas_call(
        late_kernel,
        out_shape=jax.ShapeDtypeStruct((planes, len(near), *near[0].shape[1:]), near[0].dtype),
        in_specs=[VMEM] * len(near),
        out_specs=VMEM,
        compiler_params=pltpu.CompilerParams(vmem_limit_bytes=8 * 2**20),
    )(*near)


def early_kernel(*refs):
    far, early = refs[:-NEAR], refs[-NEAR:]
    for s, ref in zip(in_turn(len(far)), far):
        for d in range(NEAR):
            early[d][s] = ref[d]


def early_blocks(far):
    return pl.pallas_call(
        early_kernel,
        out_shape=[jax.ShapeDtypeStruct((len(far), *far[0].shape[1:]), far[0].dtype)] * NEAR,
        in_specs=[VMEM] * len(far),
        out_specs=[VMEM] * NEAR,
        compiler_params=pltpu.CompilerParams(vmem_limit_bytes=8 * 2**20),
        cost_estimate=pl.CostEstimate(flops=EARLY_COST * 10**9, bytes_accessed=2**10, transcendentals=0),
    )(*far)


def all_levels(source, tables, picks, state, rhs):
    tiles, _, rank, _ = state.shape
    level_count, rows, _ = tables.shape
    table_count = rows // rank
    for level in range(level_count):
        apart = tiles >> (level + 1)
        before = source if level == 0 else lambda tile, r: state[tile, r]
        for low in range(tiles):
            if low & apart:
                continue
            pair = (low, low + apart)
            joined = jnp.concatenate(
                [jnp.concatenate([before(tile, r) for tile in pair], axis=0) for r in range(rhs)], axis=1
            )
            product = jnp.dot(tables[level], joined, preferred_element_type=jnp.float32)
            product = product.reshape(table_count, rank // 8, 8, rhs * LANES)
            for tile in pair:
                pick = jnp.broadcast_to(picks[tile, level : level + 1, :], (8, LANES))
                pick = jnp.concatenate([pick] * rhs, axis=1)
                choices = [product[t] for t in range(table_count)]
                bit = 1
                while len(choices) > 1:
                    odd = (pick & bit) != 0
                    choices = [jnp.where(odd, b, a) for a, b in zip(choices[::2], choices[1::2])]
                    bit *= 2
                chosen = choices[0].reshape(rank, rhs * LANES).astype(jnp.bfloat16)
                for r in range(rhs):
                    state[tile, r] = chosen[:, r * LANES : (r + 1) * LANES]


def flat_rows(state):
    tiles, rhs, rank, _ = state.shape
    return jnp.concatenate([state[tile].reshape(rhs * rank, LANES) for tile in range(tiles)], axis=1)


def ones_at(order, start):
    source = lax.broadcasted_iota(jnp.int32, (order.shape[1], STRIP), 0)
    return jnp.where(source == order[:, start : start + STRIP], 1.0, 0.0).astype(jnp.bfloat16)


def put(flat, hot, placed, start):
    strip = jnp.dot(flat, hot, preferred_element_type=jnp.float32).astype(jnp.bfloat16)
    placed[:, :, start : start + STRIP] = strip.reshape(*placed.shape[:2], STRIP)


def whole_kernel(received, tables, picks, order, out, state):
    all_levels(lambda tile, r: received[tile, r], tables, picks, state, received.shape[1])
    flat = flat_rows(state)
    for start in range(0, out.shape[2], STRIP):
        put(flat, ones_at(order, start), out, start)


def run_whole(received, tables, picks, order):
    tiles, rhs, rank, _ = received.shape
    return pl.pallas_call(
        whole_kernel,
        out_shape=jax.ShapeDtypeStruct((rhs, rank, tiles * LANES), jnp.bfloat16),
        in_specs=[VMEM] * 4,
        out_specs=VMEM,
        scratch_shapes=[pltpu.VMEM(received.shape, jnp.bfloat16)],
        compiler_params=pltpu.CompilerParams(vmem_limit_bytes=40 * 2**20),
    )(received, tables, picks, order)


def first_kernel(me, tables, picks, order, *refs):
    near, (placed, state) = refs[:-2], refs[-2:]
    for d, ref in zip(in_turn(NEAR), near):
        for s in range(ref.shape[0]):
            state[me[0] ^ (s * NEAR + d)] = ref[s]
    all_levels(lambda tile, r: state[tile, r], tables, picks, state, state.shape[1])
    flat = flat_rows(state)
    for start in range(0, placed.shape[2], STRIP):
        put(flat, ones_at(order, start), placed, start)


def run_first(me, tables, picks, order, near):
    planes, rhs, rank, _ = near[0].shape
    tiles = planes * len(near)
    return pl.pallas_call(
        first_kernel,
        out_shape=jax.ShapeDtypeStruct((rhs, rank, tiles * LANES), jnp.bfloat16),
        in_specs=[SMEM] + [VMEM] * (3 + len(near)),
        out_specs=VMEM,
        scratch_shapes=[pltpu.VMEM((tiles, rhs, rank, LANES), jnp.bfloat16)],
        compiler_params=pltpu.CompilerParams(vmem_limit_bytes=FIRST_VMEM),
        cost_estimate=pl.CostEstimate(flops=FIRST_COST * 10**9, bytes_accessed=2**10, transcendentals=0),
    )(me, tables, picks, order, *near)


def last_kernel(me, tables, picks, order, done, late, out, state, placed, sem):
    early, rhs = done.shape[0], out.shape[0]
    copies = [pltpu.make_async_copy(done, out.at[0:early], sem.at[0])]
    copies[0].start()
    for z in range(late.shape[0]):
        for d in range(NEAR):
            state[z * NEAR + ((me[0] % NEAR) ^ d)] = late[z, d]
    all_levels(lambda tile, r: state[tile, r], tables, picks, state, state.shape[1])
    flat = flat_rows(state)
    for number, start in enumerate(range(0, out.shape[2], STRIP)):
        columns = slice(start, start + STRIP)
        put(flat, ones_at(order, start), placed, start)
        copy = pltpu.make_async_copy(placed.at[:, :, columns], out.at[early:rhs, :, columns], sem.at[1 + number])
        copy.start()
        copies.append(copy)
    for copy in copies:
        copy.wait()


def run_last(me, tables, picks, order, done, late):
    early, rank, boxes = done.shape
    tiles, more = boxes // LANES, late.shape[2]
    return pl.pallas_call(
        last_kernel,
        out_shape=jax.ShapeDtypeStruct((early + more, rank, boxes), jnp.bfloat16),
        in_specs=[SMEM] + [VMEM] * 5,
        out_specs=pl.BlockSpec(memory_space=pl.ANY),
        scratch_shapes=[
            pltpu.VMEM((tiles, more, rank, LANES), jnp.bfloat16),
            pltpu.VMEM((more, rank, boxes), jnp.bfloat16),
            pltpu.SemaphoreType.DMA((1 + boxes // STRIP,)),
        ],
        compiler_params=pltpu.CompilerParams(vmem_limit_bytes=LAST_VMEM),
        cost_estimate=pl.CostEstimate(flops=5 * 10**9, bytes_accessed=2 * 2**20, transcendentals=0),
    )(me, tables, picks, order, done, late)


def across(block, distance):
    if distance == 0:
        return block
    count = lax.axis_size("box")
    return lax.ppermute(block, "box", [(i, i ^ distance) for i in range(count)])


def body(coeffs, operators, pattern, owner_order):
    device_count = lax.axis_size("box")
    device_index = lax.axis_index("box")
    rhs, rank, boxes = coeffs.shape
    level_count, table_count = operators.shape[:2]
    piece = boxes // device_count
    tiles = boxes // LANES
    me = device_index.reshape(1).astype(jnp.int32)
    order = owner_order.reshape(1, boxes)
    tables = operators.reshape(level_count, table_count * rank, 2 * rank)

    if piece != LANES:
        picks = pattern.reshape(level_count, device_count, device_count, piece)
        picks = lax.dynamic_index_in_dim(picks, device_index, 2, keepdims=False)
        picks = picks.reshape(level_count, tiles, LANES).transpose(1, 0, 2)
        sent = coeffs.reshape(rhs, rank, device_count, piece).transpose(2, 0, 1, 3)
        received = lax.all_to_all(sent, "box", split_axis=0, concat_axis=0, tiled=True)
        received = received.reshape(tiles, device_count // tiles, rhs, rank, piece)
        received = received.transpose(0, 2, 3, 1, 4).reshape(tiles, rhs, rank, LANES)
        return run_whole(received, tables, picks, order)

    (tables, picks), near, far = pack(me, coeffs, tables, pattern, EARLY)
    planes = len(far)
    far = [across(far[s], s * NEAR) for s in in_turn(planes)]
    near = [across(near[d], d) for d in in_turn(NEAR)]
    columns = [[z * NEAR + d for z in range(planes)] for d in range(NEAR)]
    late = lax.all_to_all(late_blocks(near), "box", 0, 0, tiled=True, axis_index_groups=columns)
    early = early_blocks(far)
    early = [across(early[d], d) for d in in_turn(NEAR)]
    done = run_first(me, tables, picks, order, early)
    return run_last(me, tables, picks, order, done, late)


def solution(mesh):
    return jax.shard_map(
        body,
        mesh=mesh,
        in_specs=(P(None, None, ("groups", "box")), P(), P(None, "groups"), P(("groups", "box"))),
        out_specs=P(None, None, ("groups", "box")),
        check_vma=False,
    )
```

```python
import functools

import jax
import jax.numpy as jnp
from jax import lax
from jax.experimental import pallas as pl
from jax.experimental.pallas import tpu as pltpu
from jax.sharding import PartitionSpec as P

LANES = 128
STRIP = 512
EARLY = 2
NEAR = 4
PACK_VMEM = 52 * 2**20
EARLY_COST = 16
FIRST_COST = 2
FETCH_COST = 1
FIRST_VMEM = 24 * 2**20
LAST_VMEM = 24 * 2**20
VMEM = pl.BlockSpec(memory_space=pltpu.VMEM)
SMEM = pl.BlockSpec(memory_space=pltpu.SMEM)


def in_turn(count):
    return [0] + list(range(max(count // 2, 1), count)) + list(range(1, count // 2))


def pack_kernel(early, me, coeffs, *refs):
    refs, sem = refs[:-1], refs[-1]
    near, far = refs[:NEAR], refs[NEAR:]
    rhs = coeffs.shape[0]
    copies = []
    for s in range(len(far)):
        for d in range(NEAR):
            tile = me[0] ^ (s * NEAR + d)
            lanes = pl.ds(pl.multiple_of(tile * LANES, LANES), LANES)
            copies.append((coeffs.at[0:early, :, lanes], far[s].at[d]))
            tile = s * NEAR + ((me[0] % NEAR) ^ d)
            lanes = pl.ds(pl.multiple_of(tile * LANES, LANES), LANES)
            copies.append((coeffs.at[early:rhs, :, lanes], near[d].at[s]))
    copies = [pltpu.make_async_copy(a, b, sem.at[n]) for n, (a, b) in enumerate(copies)]
    for copy in copies:
        copy.start()
    for copy in copies:
        copy.wait()


def pack(me, coeffs, early):
    rhs, rank, boxes = coeffs.shape
    tiles = boxes // LANES
    planes = tiles // NEAR
    shapes = [(planes, rhs - early, rank, LANES)] * NEAR + [(NEAR, early, rank, LANES)] * planes
    packed = pl.pallas_call(
        functools.partial(pack_kernel, early),
        out_shape=[jax.ShapeDtypeStruct(s, coeffs.dtype) for s in shapes],
        in_specs=[SMEM, pl.BlockSpec(memory_space=pl.ANY)],
        out_specs=[VMEM] * len(shapes),
        scratch_shapes=[pltpu.SemaphoreType.DMA((2 * tiles,))],
        compiler_params=pltpu.CompilerParams(vmem_limit_bytes=PACK_VMEM),
    )(me, coeffs)
    return packed[:NEAR], packed[NEAR:]


def fetch_kernel(me, operators, pattern, tables, picks, sem):
    boxes = pattern.shape[1] // picks.shape[0]
    copies = [(operators, tables)]
    for tile in range(picks.shape[0]):
        lanes = pl.ds(pl.multiple_of(tile * boxes + me[0] * LANES, LANES), LANES)
        copies.append((pattern.at[:, lanes], picks.at[tile]))
    copies = [pltpu.make_async_copy(a, b, sem.at[n]) for n, (a, b) in enumerate(copies)]
    for copy in copies:
        copy.start()
    for copy in copies:
        copy.wait()


def fetch(me, operators, pattern, tiles):
    return pl.pallas_call(
        fetch_kernel,
        out_shape=[
            jax.ShapeDtypeStruct(operators.shape, operators.dtype),
            jax.ShapeDtypeStruct((tiles, pattern.shape[0], LANES), pattern.dtype),
        ],
        in_specs=[SMEM] + [pl.BlockSpec(memory_space=pl.ANY)] * 2,
        out_specs=[VMEM] * 2,
        scratch_shapes=[pltpu.SemaphoreType.DMA((1 + tiles,))],
        compiler_params=pltpu.CompilerParams(vmem_limit_bytes=PACK_VMEM),
        cost_estimate=pl.CostEstimate(flops=FETCH_COST * 10**9, bytes_accessed=2**10, transcendentals=0),
    )(me, operators, pattern)


def late_kernel(*refs):
    near, late = refs[:-1], refs[-1]
    for d, ref in zip(in_turn(NEAR), near):
        for z in range(late.shape[0]):
            late[z, d] = ref[z]


def late_blocks(near):
    planes = near[0].shape[0]
    return pl.pallas_call(
        late_kernel,
        out_shape=jax.ShapeDtypeStruct((planes, len(near), *near[0].shape[1:]), near[0].dtype),
        in_specs=[VMEM] * len(near),
        out_specs=VMEM,
        compiler_params=pltpu.CompilerParams(vmem_limit_bytes=8 * 2**20),
    )(*near)


def early_kernel(*refs):
    far, early = refs[:-NEAR], refs[-NEAR:]
    for s, ref in zip(in_turn(len(far)), far):
        for d in range(NEAR):
            early[d][s] = ref[d]


def early_blocks(far):
    return pl.pallas_call(
        early_kernel,
        out_shape=[jax.ShapeDtypeStruct((len(far), *far[0].shape[1:]), far[0].dtype)] * NEAR,
        in_specs=[VMEM] * len(far),
        out_specs=[VMEM] * NEAR,
        compiler_params=pltpu.CompilerParams(vmem_limit_bytes=8 * 2**20),
        cost_estimate=pl.CostEstimate(flops=EARLY_COST * 10**9, bytes_accessed=2**10, transcendentals=0),
    )(*far)


def all_levels(source, tables, picks, state, rhs):
    tiles, _, rank, _ = state.shape
    level_count, rows, _ = tables.shape
    table_count = rows // rank
    for level in range(level_count):
        apart = tiles >> (level + 1)
        before = source if level == 0 else lambda tile, r: state[tile, r]
        for low in range(tiles):
            if low & apart:
                continue
            pair = (low, low + apart)
            joined = jnp.concatenate(
                [jnp.concatenate([before(tile, r) for tile in pair], axis=0) for r in range(rhs)], axis=1
            )
            product = jnp.dot(tables[level], joined, preferred_element_type=jnp.float32)
            product = product.reshape(table_count, rank // 8, 8, rhs * LANES)
            for tile in pair:
                pick = jnp.broadcast_to(picks[tile, level : level + 1, :], (8, LANES))
                pick = jnp.concatenate([pick] * rhs, axis=1)
                choices = [product[t] for t in range(table_count)]
                bit = 1
                while len(choices) > 1:
                    odd = (pick & bit) != 0
                    choices = [jnp.where(odd, b, a) for a, b in zip(choices[::2], choices[1::2])]
                    bit *= 2
                chosen = choices[0].reshape(rank, rhs * LANES).astype(jnp.bfloat16)
                for r in range(rhs):
                    state[tile, r] = chosen[:, r * LANES : (r + 1) * LANES]


def flat_rows(state):
    tiles, rhs, rank, _ = state.shape
    return jnp.concatenate([state[tile].reshape(rhs * rank, LANES) for tile in range(tiles)], axis=1)


def ones_at(order, start):
    source = lax.broadcasted_iota(jnp.int32, (order.shape[1], STRIP), 0)
    return jnp.where(source == order[:, start : start + STRIP], 1.0, 0.0).astype(jnp.bfloat16)


def put(flat, hot, placed, start):
    strip = jnp.dot(flat, hot, preferred_element_type=jnp.float32).astype(jnp.bfloat16)
    placed[:, :, start : start + STRIP] = strip.reshape(*placed.shape[:2], STRIP)


def whole_kernel(received, tables, picks, order, out, state):
    all_levels(lambda tile, r: received[tile, r], tables, picks, state, received.shape[1])
    flat = flat_rows(state)
    for start in range(0, out.shape[2], STRIP):
        put(flat, ones_at(order, start), out, start)


def run_whole(received, tables, picks, order):
    tiles, rhs, rank, _ = received.shape
    return pl.pallas_call(
        whole_kernel,
        out_shape=jax.ShapeDtypeStruct((rhs, rank, tiles * LANES), jnp.bfloat16),
        in_specs=[VMEM] * 4,
        out_specs=VMEM,
        scratch_shapes=[pltpu.VMEM(received.shape, jnp.bfloat16)],
        compiler_params=pltpu.CompilerParams(vmem_limit_bytes=40 * 2**20),
    )(received, tables, picks, order)


def first_kernel(me, tables, picks, order, *refs):
    near, (placed, state) = refs[:-2], refs[-2:]
    for d, ref in zip(in_turn(NEAR), near):
        for s in range(ref.shape[0]):
            state[me[0] ^ (s * NEAR + d)] = ref[s]
    all_levels(lambda tile, r: state[tile, r], tables, picks, state, state.shape[1])
    flat = flat_rows(state)
    for start in range(0, placed.shape[2], STRIP):
        put(flat, ones_at(order, start), placed, start)


def run_first(me, tables, picks, order, near):
    planes, rhs, rank, _ = near[0].shape
    tiles = planes * len(near)
    return pl.pallas_call(
        first_kernel,
        out_shape=jax.ShapeDtypeStruct((rhs, rank, tiles * LANES), jnp.bfloat16),
        in_specs=[SMEM] + [VMEM] * (3 + len(near)),
        out_specs=VMEM,
        scratch_shapes=[pltpu.VMEM((tiles, rhs, rank, LANES), jnp.bfloat16)],
        compiler_params=pltpu.CompilerParams(vmem_limit_bytes=FIRST_VMEM),
        cost_estimate=pl.CostEstimate(flops=FIRST_COST * 10**9, bytes_accessed=2**10, transcendentals=0),
    )(me, tables, picks, order, *near)


def last_kernel(me, tables, picks, order, done, late, out, state, placed, sem):
    early, rhs = done.shape[0], out.shape[0]
    copies = [pltpu.make_async_copy(done, out.at[0:early], sem.at[0])]
    copies[0].start()
    for z in range(late.shape[0]):
        for d in range(NEAR):
            state[z * NEAR + ((me[0] % NEAR) ^ d)] = late[z, d]
    all_levels(lambda tile, r: state[tile, r], tables, picks, state, state.shape[1])
    flat = flat_rows(state)
    for number, start in enumerate(range(0, out.shape[2], STRIP)):
        columns = slice(start, start + STRIP)
        put(flat, ones_at(order, start), placed, start)
        copy = pltpu.make_async_copy(placed.at[:, :, columns], out.at[early:rhs, :, columns], sem.at[1 + number])
        copy.start()
        copies.append(copy)
    for copy in copies:
        copy.wait()


def run_last(me, tables, picks, order, done, late):
    early, rank, boxes = done.shape
    tiles, more = boxes // LANES, late.shape[2]
    return pl.pallas_call(
        last_kernel,
        out_shape=jax.ShapeDtypeStruct((early + more, rank, boxes), jnp.bfloat16),
        in_specs=[SMEM] + [VMEM] * 5,
        out_specs=pl.BlockSpec(memory_space=pl.ANY),
        scratch_shapes=[
            pltpu.VMEM((tiles, more, rank, LANES), jnp.bfloat16),
            pltpu.VMEM((more, rank, boxes), jnp.bfloat16),
            pltpu.SemaphoreType.DMA((1 + boxes // STRIP,)),
        ],
        compiler_params=pltpu.CompilerParams(vmem_limit_bytes=LAST_VMEM),
        cost_estimate=pl.CostEstimate(flops=5 * 10**9, bytes_accessed=2 * 2**20, transcendentals=0),
    )(me, tables, picks, order, done, late)


def across(block, distance):
    if distance == 0:
        return block
    count = lax.axis_size("box")
    return lax.ppermute(block, "box", [(i, i ^ distance) for i in range(count)])


def body(coeffs, operators, pattern, owner_order):
    device_count = lax.axis_size("box")
    device_index = lax.axis_index("box")
    rhs, rank, boxes = coeffs.shape
    level_count, table_count = operators.shape[:2]
    piece = boxes // device_count
    tiles = boxes // LANES
    me = device_index.reshape(1).astype(jnp.int32)
    order = owner_order.reshape(1, boxes)
    tables = operators.reshape(level_count, table_count * rank, 2 * rank)

    if piece != LANES:
        picks = pattern.reshape(level_count, device_count, device_count, piece)
        picks = lax.dynamic_index_in_dim(picks, device_index, 2, keepdims=False)
        picks = picks.reshape(level_count, tiles, LANES).transpose(1, 0, 2)
        sent = coeffs.reshape(rhs, rank, device_count, piece).transpose(2, 0, 1, 3)
        received = lax.all_to_all(sent, "box", split_axis=0, concat_axis=0, tiled=True)
        received = received.reshape(tiles, device_count // tiles, rhs, rank, piece)
        received = received.transpose(0, 2, 3, 1, 4).reshape(tiles, rhs, rank, LANES)
        return run_whole(received, tables, picks, order)

    near, far = pack(me, coeffs, EARLY)
    tables, picks = fetch(me, tables, pattern, tiles)
    planes = len(far)
    far = [across(far[s], s * NEAR) for s in in_turn(planes)]
    near = [across(near[d], d) for d in in_turn(NEAR)]
    columns = [[z * NEAR + d for z in range(planes)] for d in range(NEAR)]
    late = lax.all_to_all(late_blocks(near), "box", 0, 0, tiled=True, axis_index_groups=columns)
    early = early_blocks(far)
    early = [across(early[d], d) for d in in_turn(NEAR)]
    done = run_first(me, tables, picks, order, early)
    return run_last(me, tables, picks, order, done, late)


def solution(mesh):
    return jax.shard_map(
        body,
        mesh=mesh,
        in_specs=(P(None, None, ("groups", "box")), P(), P(None, "groups"), P(("groups", "box"))),
        out_specs=P(None, None, ("groups", "box")),
        check_vma=False,
    )
```

```python
import functools

import jax
import jax.numpy as jnp
from jax import lax
from jax.experimental import pallas as pl
from jax.experimental.pallas import tpu as pltpu
from jax.sharding import PartitionSpec as P

LANES = 128
STRIP = 512
EARLY = 2
NEAR = 4
PACK_VMEM = 52 * 2**20
EARLY_COST = 16
FIRST_COST = 2
FETCH_COST = 1
FIRST_VMEM = 24 * 2**20
LAST_VMEM = 24 * 2**20
VMEM = pl.BlockSpec(memory_space=pltpu.VMEM)
SMEM = pl.BlockSpec(memory_space=pltpu.SMEM)


def in_turn(count):
    return [0] + list(range(max(count // 2, 1), count)) + list(range(1, count // 2))


def pack_kernel(early, me, coeffs, *refs):
    refs, sem = refs[:-1], refs[-1]
    near, far = refs[:NEAR], refs[NEAR:]
    rhs = coeffs.shape[0]
    copies = []
    for s in range(len(far)):
        for d in range(NEAR):
            tile = me[0] ^ (s * NEAR + d)
            lanes = pl.ds(pl.multiple_of(tile * LANES, LANES), LANES)
            copies.append((coeffs.at[0:early, :, lanes], far[s].at[d]))
            tile = s * NEAR + ((me[0] % NEAR) ^ d)
            lanes = pl.ds(pl.multiple_of(tile * LANES, LANES), LANES)
            copies.append((coeffs.at[early:rhs, :, lanes], near[d].at[s]))
    copies = [pltpu.make_async_copy(a, b, sem.at[n]) for n, (a, b) in enumerate(copies)]
    for copy in copies:
        copy.start()
    for copy in copies:
        copy.wait()


def pack(me, coeffs, early):
    rhs, rank, boxes = coeffs.shape
    tiles = boxes // LANES
    planes = tiles // NEAR
    shapes = [(planes, rhs - early, rank, LANES)] * NEAR + [(NEAR, early, rank, LANES)] * planes
    packed = pl.pallas_call(
        functools.partial(pack_kernel, early),
        out_shape=[jax.ShapeDtypeStruct(s, coeffs.dtype) for s in shapes],
        in_specs=[SMEM, pl.BlockSpec(memory_space=pl.ANY)],
        out_specs=[VMEM] * len(shapes),
        scratch_shapes=[pltpu.SemaphoreType.DMA((2 * tiles,))],
        compiler_params=pltpu.CompilerParams(vmem_limit_bytes=PACK_VMEM),
    )(me, coeffs)
    return packed[:NEAR], packed[NEAR:]


def fetch_kernel(me, operators, pattern, tables, picks, sem):
    boxes = pattern.shape[1] // picks.shape[0]
    copies = [(operators, tables)]
    for tile in range(picks.shape[0]):
        lanes = pl.ds(pl.multiple_of(tile * boxes + me[0] * LANES, LANES), LANES)
        copies.append((pattern.at[:, lanes], picks.at[tile]))
    copies = [pltpu.make_async_copy(a, b, sem.at[n]) for n, (a, b) in enumerate(copies)]
    for copy in copies:
        copy.start()
    for copy in copies:
        copy.wait()


def fetch(me, operators, pattern, tiles):
    return pl.pallas_call(
        fetch_kernel,
        out_shape=[
            jax.ShapeDtypeStruct(operators.shape, operators.dtype),
            jax.ShapeDtypeStruct((tiles, pattern.shape[0], LANES), pattern.dtype),
        ],
        in_specs=[SMEM] + [pl.BlockSpec(memory_space=pl.ANY)] * 2,
        out_specs=[VMEM] * 2,
        scratch_shapes=[pltpu.SemaphoreType.DMA((1 + tiles,))],
        compiler_params=pltpu.CompilerParams(vmem_limit_bytes=PACK_VMEM),
        cost_estimate=pl.CostEstimate(flops=FETCH_COST * 10**9, bytes_accessed=2**10, transcendentals=0),
    )(me, operators, pattern)


def late_kernel(*refs):
    near, late = refs[:-1], refs[-1]
    for d, ref in zip(in_turn(NEAR), near):
        for z in range(late.shape[0]):
            late[z, d] = ref[z]


def late_blocks(near):
    planes = near[0].shape[0]
    return pl.pallas_call(
        late_kernel,
        out_shape=jax.ShapeDtypeStruct((planes, len(near), *near[0].shape[1:]), near[0].dtype),
        in_specs=[VMEM] * len(near),
        out_specs=VMEM,
        compiler_params=pltpu.CompilerParams(vmem_limit_bytes=8 * 2**20),
    )(*near)


def early_kernel(*refs):
    far, early = refs[:-NEAR], refs[-NEAR:]
    for s, ref in zip(in_turn(len(far)), far):
        for d in range(NEAR):
            early[d][s] = ref[d]


def early_blocks(far):
    return pl.pallas_call(
        early_kernel,
        out_shape=[jax.ShapeDtypeStruct((len(far), *far[0].shape[1:]), far[0].dtype)] * NEAR,
        in_specs=[VMEM] * len(far),
        out_specs=[VMEM] * NEAR,
        compiler_params=pltpu.CompilerParams(vmem_limit_bytes=8 * 2**20),
        cost_estimate=pl.CostEstimate(flops=EARLY_COST * 10**9, bytes_accessed=2**10, transcendentals=0),
    )(*far)


def all_levels(source, tables, picks, state, rhs):
    tiles, _, rank, _ = state.shape
    level_count, rows, _ = tables.shape
    table_count = rows // rank
    for level in range(level_count):
        apart = tiles >> (level + 1)
        before = source if level == 0 else lambda tile, r: state[tile, r]
        for low in range(tiles):
            if low & apart:
                continue
            pair = (low, low + apart)
            joined = jnp.concatenate(
                [jnp.concatenate([before(tile, r) for tile in pair], axis=0) for r in range(rhs)], axis=1
            )
            product = jnp.dot(tables[level], joined, preferred_element_type=jnp.float32)
            product = product.astype(jnp.bfloat16).reshape(table_count, rank // 16, 16, rhs * LANES)
            for tile in pair:
                pick = jnp.broadcast_to(picks[tile, level : level + 1, :], (16, LANES)).astype(jnp.int16)
                pick = jnp.concatenate([pick] * rhs, axis=1)
                choices = [product[t] for t in range(table_count)]
                bit = 1
                while len(choices) > 1:
                    odd = (pick & jnp.int16(bit)) != jnp.int16(0)
                    choices = [jnp.where(odd, b, a) for a, b in zip(choices[::2], choices[1::2])]
                    bit *= 2
                chosen = choices[0].reshape(rank, rhs * LANES)
                for r in range(rhs):
                    state[tile, r] = chosen[:, r * LANES : (r + 1) * LANES]


def flat_rows(state):
    tiles, rhs, rank, _ = state.shape
    return jnp.concatenate([state[tile].reshape(rhs * rank, LANES) for tile in range(tiles)], axis=1)


def ones_at(order, start):
    source = lax.broadcasted_iota(jnp.int32, (order.shape[1], STRIP), 0)
    return jnp.where(source == order[:, start : start + STRIP], 1.0, 0.0).astype(jnp.bfloat16)


def put(flat, hot, placed, start):
    strip = jnp.dot(flat, hot, preferred_element_type=jnp.float32).astype(jnp.bfloat16)
    placed[:, :, start : start + STRIP] = strip.reshape(*placed.shape[:2], STRIP)


def whole_kernel(received, tables, picks, order, out, state):
    all_levels(lambda tile, r: received[tile, r], tables, picks, state, received.shape[1])
    flat = flat_rows(state)
    for start in range(0, out.shape[2], STRIP):
        put(flat, ones_at(order, start), out, start)


def run_whole(received, tables, picks, order):
    tiles, rhs, rank, _ = received.shape
    return pl.pallas_call(
        whole_kernel,
        out_shape=jax.ShapeDtypeStruct((rhs, rank, tiles * LANES), jnp.bfloat16),
        in_specs=[VMEM] * 4,
        out_specs=VMEM,
        scratch_shapes=[pltpu.VMEM(received.shape, jnp.bfloat16)],
        compiler_params=pltpu.CompilerParams(vmem_limit_bytes=40 * 2**20),
    )(received, tables, picks, order)


def first_kernel(me, tables, picks, order, *refs):
    near, (placed, state) = refs[:-2], refs[-2:]
    for d, ref in zip(in_turn(NEAR), near):
        for s in range(ref.shape[0]):
            state[me[0] ^ (s * NEAR + d)] = ref[s]
    all_levels(lambda tile, r: state[tile, r], tables, picks, state, state.shape[1])
    flat = flat_rows(state)
    for start in range(0, placed.shape[2], STRIP):
        put(flat, ones_at(order, start), placed, start)


def run_first(me, tables, picks, order, near):
    planes, rhs, rank, _ = near[0].shape
    tiles = planes * len(near)
    return pl.pallas_call(
        first_kernel,
        out_shape=jax.ShapeDtypeStruct((rhs, rank, tiles * LANES), jnp.bfloat16),
        in_specs=[SMEM] + [VMEM] * (3 + len(near)),
        out_specs=VMEM,
        scratch_shapes=[pltpu.VMEM((tiles, rhs, rank, LANES), jnp.bfloat16)],
        compiler_params=pltpu.CompilerParams(vmem_limit_bytes=FIRST_VMEM),
        cost_estimate=pl.CostEstimate(flops=FIRST_COST * 10**9, bytes_accessed=2**10, transcendentals=0),
    )(me, tables, picks, order, *near)


def last_kernel(me, tables, picks, order, done, late, out, state, placed, sem):
    early, rhs = done.shape[0], out.shape[0]
    copies = [pltpu.make_async_copy(done, out.at[0:early], sem.at[0])]
    copies[0].start()
    own = me[0] % NEAR
    arrived = lambda tile, r: late[tile // NEAR, (tile % NEAR) ^ own, r]
    all_levels(arrived, tables, picks, state, state.shape[1])
    flat = flat_rows(state)
    for number, start in enumerate(range(0, out.shape[2], STRIP)):
        columns = slice(start, start + STRIP)
        put(flat, ones_at(order, start), placed, start)
        copy = pltpu.make_async_copy(placed.at[:, :, columns], out.at[early:rhs, :, columns], sem.at[1 + number])
        copy.start()
        copies.append(copy)
    for copy in copies:
        copy.wait()


def run_last(me, tables, picks, order, done, late):
    early, rank, boxes = done.shape
    tiles, more = boxes // LANES, late.shape[2]
    return pl.pallas_call(
        last_kernel,
        out_shape=jax.ShapeDtypeStruct((early + more, rank, boxes), jnp.bfloat16),
        in_specs=[SMEM] + [VMEM] * 5,
        out_specs=pl.BlockSpec(memory_space=pl.ANY),
        scratch_shapes=[
            pltpu.VMEM((tiles, more, rank, LANES), jnp.bfloat16),
            pltpu.VMEM((more, rank, boxes), jnp.bfloat16),
            pltpu.SemaphoreType.DMA((1 + boxes // STRIP,)),
        ],
        compiler_params=pltpu.CompilerParams(vmem_limit_bytes=LAST_VMEM),
        cost_estimate=pl.CostEstimate(flops=5 * 10**9, bytes_accessed=2 * 2**20, transcendentals=0),
    )(me, tables, picks, order, done, late)


def across(block, distance):
    if distance == 0:
        return block
    count = lax.axis_size("box")
    return lax.ppermute(block, "box", [(i, i ^ distance) for i in range(count)])


def body(coeffs, operators, pattern, owner_order):
    device_count = lax.axis_size("box")
    device_index = lax.axis_index("box")
    rhs, rank, boxes = coeffs.shape
    level_count, table_count = operators.shape[:2]
    piece = boxes // device_count
    tiles = boxes // LANES
    me = device_index.reshape(1).astype(jnp.int32)
    order = owner_order.reshape(1, boxes)
    tables = operators.reshape(level_count, table_count * rank, 2 * rank)

    if piece != LANES:
        picks = pattern.reshape(level_count, device_count, device_count, piece)
        picks = lax.dynamic_index_in_dim(picks, device_index, 2, keepdims=False)
        picks = picks.reshape(level_count, tiles, LANES).transpose(1, 0, 2)
        sent = coeffs.reshape(rhs, rank, device_count, piece).transpose(2, 0, 1, 3)
        received = lax.all_to_all(sent, "box", split_axis=0, concat_axis=0, tiled=True)
        received = received.reshape(tiles, device_count // tiles, rhs, rank, piece)
        received = received.transpose(0, 2, 3, 1, 4).reshape(tiles, rhs, rank, LANES)
        return run_whole(received, tables, picks, order)

    near, far = pack(me, coeffs, EARLY)
    tables, picks = fetch(me, tables, pattern, tiles)
    planes = len(far)
    far = [across(far[s], s * NEAR) for s in in_turn(planes)]
    near = [across(near[d], d) for d in in_turn(NEAR)]
    columns = [[z * NEAR + d for z in range(planes)] for d in range(NEAR)]
    late = lax.all_to_all(late_blocks(near), "box", 0, 0, tiled=True, axis_index_groups=columns)
    early = early_blocks(far)
    early = [across(early[d], d) for d in in_turn(NEAR)]
    done = run_first(me, tables, picks, order, early)
    return run_last(me, tables, picks, order, done, late)


def solution(mesh):
    return jax.shard_map(
        body,
        mesh=mesh,
        in_specs=(P(None, None, ("groups", "box")), P(), P(None, "groups"), P(("groups", "box"))),
        out_specs=P(None, None, ("groups", "box")),
        check_vma=False,
    )
```

```python
import functools

import jax
import jax.numpy as jnp
from jax import lax
from jax.experimental import pallas as pl
from jax.experimental.pallas import tpu as pltpu
from jax.sharding import PartitionSpec as P

LANES = 128
STRIP = 512
EARLY = 2
NEAR = 4
PACK_VMEM = 52 * 2**20
EARLY_COST = 16
FIRST_COST = 2
FETCH_COST = 1
FIRST_VMEM = 24 * 2**20
LAST_VMEM = 24 * 2**20
VMEM = pl.BlockSpec(memory_space=pltpu.VMEM)
SMEM = pl.BlockSpec(memory_space=pltpu.SMEM)


def in_turn(count):
    return [0] + list(range(max(count // 2, 1), count)) + list(range(1, count // 2))


def mixed(count):
    turns = in_turn(count)
    far, close = turns[1 : 1 + count - max(count // 2, 1)], turns[1 + count - max(count // 2, 1) :]
    order = [0]
    for n in range(len(far)):
        order += far[n : n + 1] + close[n : n + 1]
    return order


def pack_kernel(early, me, coeffs, *refs):
    refs, sem = refs[:-1], refs[-1]
    near, far = refs[:NEAR], refs[NEAR:]
    rhs = coeffs.shape[0]
    copies = []
    for s in range(len(far)):
        for d in range(NEAR):
            tile = me[0] ^ (s * NEAR + d)
            lanes = pl.ds(pl.multiple_of(tile * LANES, LANES), LANES)
            copies.append((coeffs.at[0:early, :, lanes], far[s].at[d]))
            tile = s * NEAR + ((me[0] % NEAR) ^ d)
            lanes = pl.ds(pl.multiple_of(tile * LANES, LANES), LANES)
            copies.append((coeffs.at[early:rhs, :, lanes], near[d].at[s]))
    copies = [pltpu.make_async_copy(a, b, sem.at[n]) for n, (a, b) in enumerate(copies)]
    for copy in copies:
        copy.start()
    for copy in copies:
        copy.wait()


def pack(me, coeffs, early):
    rhs, rank, boxes = coeffs.shape
    tiles = boxes // LANES
    planes = tiles // NEAR
    shapes = [(planes, rhs - early, rank, LANES)] * NEAR + [(NEAR, early, rank, LANES)] * planes
    packed = pl.pallas_call(
        functools.partial(pack_kernel, early),
        out_shape=[jax.ShapeDtypeStruct(s, coeffs.dtype) for s in shapes],
        in_specs=[SMEM, pl.BlockSpec(memory_space=pl.ANY)],
        out_specs=[VMEM] * len(shapes),
        scratch_shapes=[pltpu.SemaphoreType.DMA((2 * tiles,))],
        compiler_params=pltpu.CompilerParams(vmem_limit_bytes=PACK_VMEM),
    )(me, coeffs)
    return packed[:NEAR], packed[NEAR:]


def fetch_kernel(me, operators, pattern, tables, picks, sem):
    boxes = pattern.shape[1] // picks.shape[0]
    copies = [(operators, tables)]
    for tile in range(picks.shape[0]):
        lanes = pl.ds(pl.multiple_of(tile * boxes + me[0] * LANES, LANES), LANES)
        copies.append((pattern.at[:, lanes], picks.at[tile]))
    copies = [pltpu.make_async_copy(a, b, sem.at[n]) for n, (a, b) in enumerate(copies)]
    for copy in copies:
        copy.start()
    for copy in copies:
        copy.wait()


def fetch(me, operators, pattern, tiles):
    return pl.pallas_call(
        fetch_kernel,
        out_shape=[
            jax.ShapeDtypeStruct(operators.shape, operators.dtype),
            jax.ShapeDtypeStruct((tiles, pattern.shape[0], LANES), pattern.dtype),
        ],
        in_specs=[SMEM] + [pl.BlockSpec(memory_space=pl.ANY)] * 2,
        out_specs=[VMEM] * 2,
        scratch_shapes=[pltpu.SemaphoreType.DMA((1 + tiles,))],
        compiler_params=pltpu.CompilerParams(vmem_limit_bytes=PACK_VMEM),
        cost_estimate=pl.CostEstimate(flops=FETCH_COST * 10**9, bytes_accessed=2**10, transcendentals=0),
    )(me, operators, pattern)


def late_kernel(*refs):
    near, late = refs[:-1], refs[-1]
    for d, ref in zip(in_turn(NEAR), near):
        for z in range(late.shape[0]):
            late[z, d] = ref[z]


def late_blocks(near):
    planes = near[0].shape[0]
    return pl.pallas_call(
        late_kernel,
        out_shape=jax.ShapeDtypeStruct((planes, len(near), *near[0].shape[1:]), near[0].dtype),
        in_specs=[VMEM] * len(near),
        out_specs=VMEM,
        compiler_params=pltpu.CompilerParams(vmem_limit_bytes=8 * 2**20),
    )(*near)


def early_kernel(*refs):
    far, early = refs[:-NEAR], refs[-NEAR:]
    for s, ref in zip(mixed(len(far)), far):
        for d in range(NEAR):
            early[d][s] = ref[d]


def early_blocks(far):
    return pl.pallas_call(
        early_kernel,
        out_shape=[jax.ShapeDtypeStruct((len(far), *far[0].shape[1:]), far[0].dtype)] * NEAR,
        in_specs=[VMEM] * len(far),
        out_specs=[VMEM] * NEAR,
        compiler_params=pltpu.CompilerParams(vmem_limit_bytes=8 * 2**20),
        cost_estimate=pl.CostEstimate(flops=EARLY_COST * 10**9, bytes_accessed=2**10, transcendentals=0),
    )(*far)


def all_levels(source, tables, picks, state, rhs):
    tiles, _, rank, _ = state.shape
    level_count, rows, _ = tables.shape
    table_count = rows // rank
    for level in range(level_count):
        apart = tiles >> (level + 1)
        before = source if level == 0 else lambda tile, r: state[tile, r]
        for low in range(tiles):
            if low & apart:
                continue
            pair = (low, low + apart)
            joined = jnp.concatenate(
                [jnp.concatenate([before(tile, r) for tile in pair], axis=0) for r in range(rhs)], axis=1
            )
            product = jnp.dot(tables[level], joined, preferred_element_type=jnp.float32)
            product = product.astype(jnp.bfloat16).reshape(table_count, rank // 16, 16, rhs * LANES)
            for tile in pair:
                pick = jnp.broadcast_to(picks[tile, level : level + 1, :], (16, LANES)).astype(jnp.int16)
                pick = jnp.concatenate([pick] * rhs, axis=1)
                choices = [product[t] for t in range(table_count)]
                bit = 1
                while len(choices) > 1:
                    odd = (pick & jnp.int16(bit)) != jnp.int16(0)
                    choices = [jnp.where(odd, b, a) for a, b in zip(choices[::2], choices[1::2])]
                    bit *= 2
                chosen = choices[0].reshape(rank, rhs * LANES)
                for r in range(rhs):
                    state[tile, r] = chosen[:, r * LANES : (r + 1) * LANES]


def flat_rows(state):
    tiles, rhs, rank, _ = state.shape
    return jnp.concatenate([state[tile].reshape(rhs * rank, LANES) for tile in range(tiles)], axis=1)


def ones_at(order, start):
    source = lax.broadcasted_iota(jnp.int32, (order.shape[1], STRIP), 0)
    return jnp.where(source == order[:, start : start + STRIP], 1.0, 0.0).astype(jnp.bfloat16)


def put(flat, hot, placed, start):
    strip = jnp.dot(flat, hot, preferred_element_type=jnp.float32).astype(jnp.bfloat16)
    placed[:, :, start : start + STRIP] = strip.reshape(*placed.shape[:2], STRIP)


def whole_kernel(received, tables, picks, order, out, state):
    all_levels(lambda tile, r: received[tile, r], tables, picks, state, received.shape[1])
    flat = flat_rows(state)
    for start in range(0, out.shape[2], STRIP):
        put(flat, ones_at(order, start), out, start)


def run_whole(received, tables, picks, order):
    tiles, rhs, rank, _ = received.shape
    return pl.pallas_call(
        whole_kernel,
        out_shape=jax.ShapeDtypeStruct((rhs, rank, tiles * LANES), jnp.bfloat16),
        in_specs=[VMEM] * 4,
        out_specs=VMEM,
        scratch_shapes=[pltpu.VMEM(received.shape, jnp.bfloat16)],
        compiler_params=pltpu.CompilerParams(vmem_limit_bytes=40 * 2**20),
    )(received, tables, picks, order)


def first_kernel(me, tables, picks, order, *refs):
    near, (placed, state) = refs[:-2], refs[-2:]
    for d, ref in zip(in_turn(NEAR), near):
        for s in range(ref.shape[0]):
            state[me[0] ^ (s * NEAR + d)] = ref[s]
    all_levels(lambda tile, r: state[tile, r], tables, picks, state, state.shape[1])
    flat = flat_rows(state)
    for start in range(0, placed.shape[2], STRIP):
        put(flat, ones_at(order, start), placed, start)


def run_first(me, tables, picks, order, near):
    planes, rhs, rank, _ = near[0].shape
    tiles = planes * len(near)
    return pl.pallas_call(
        first_kernel,
        out_shape=jax.ShapeDtypeStruct((rhs, rank, tiles * LANES), jnp.bfloat16),
        in_specs=[SMEM] + [VMEM] * (3 + len(near)),
        out_specs=VMEM,
        scratch_shapes=[pltpu.VMEM((tiles, rhs, rank, LANES), jnp.bfloat16)],
        compiler_params=pltpu.CompilerParams(vmem_limit_bytes=FIRST_VMEM),
        cost_estimate=pl.CostEstimate(flops=FIRST_COST * 10**9, bytes_accessed=2**10, transcendentals=0),
    )(me, tables, picks, order, *near)


def last_kernel(me, tables, picks, order, done, late, out, state, placed, sem):
    early, rhs = done.shape[0], out.shape[0]
    copies = [pltpu.make_async_copy(done, out.at[0:early], sem.at[0])]
    copies[0].start()
    own = me[0] % NEAR
    arrived = lambda tile, r: late[tile // NEAR, (tile % NEAR) ^ own, r]
    all_levels(arrived, tables, picks, state, state.shape[1])
    flat = flat_rows(state)
    for number, start in enumerate(range(0, out.shape[2], STRIP)):
        columns = slice(start, start + STRIP)
        put(flat, ones_at(order, start), placed, start)
        copy = pltpu.make_async_copy(placed.at[:, :, columns], out.at[early:rhs, :, columns], sem.at[1 + number])
        copy.start()
        copies.append(copy)
    for copy in copies:
        copy.wait()


def run_last(me, tables, picks, order, done, late):
    early, rank, boxes = done.shape
    tiles, more = boxes // LANES, late.shape[2]
    return pl.pallas_call(
        last_kernel,
        out_shape=jax.ShapeDtypeStruct((early + more, rank, boxes), jnp.bfloat16),
        in_specs=[SMEM] + [VMEM] * 5,
        out_specs=pl.BlockSpec(memory_space=pl.ANY),
        scratch_shapes=[
            pltpu.VMEM((tiles, more, rank, LANES), jnp.bfloat16),
            pltpu.VMEM((more, rank, boxes), jnp.bfloat16),
            pltpu.SemaphoreType.DMA((1 + boxes // STRIP,)),
        ],
        compiler_params=pltpu.CompilerParams(vmem_limit_bytes=LAST_VMEM),
        cost_estimate=pl.CostEstimate(flops=5 * 10**9, bytes_accessed=2 * 2**20, transcendentals=0),
    )(me, tables, picks, order, done, late)


def across(block, distance):
    if distance == 0:
        return block
    count = lax.axis_size("box")
    return lax.ppermute(block, "box", [(i, i ^ distance) for i in range(count)])


def body(coeffs, operators, pattern, owner_order):
    device_count = lax.axis_size("box")
    device_index = lax.axis_index("box")
    rhs, rank, boxes = coeffs.shape
    level_count, table_count = operators.shape[:2]
    piece = boxes // device_count
    tiles = boxes // LANES
    me = device_index.reshape(1).astype(jnp.int32)
    order = owner_order.reshape(1, boxes)
    tables = operators.reshape(level_count, table_count * rank, 2 * rank)

    if piece != LANES:
        picks = pattern.reshape(level_count, device_count, device_count, piece)
        picks = lax.dynamic_index_in_dim(picks, device_index, 2, keepdims=False)
        picks = picks.reshape(level_count, tiles, LANES).transpose(1, 0, 2)
        sent = coeffs.reshape(rhs, rank, device_count, piece).transpose(2, 0, 1, 3)
        received = lax.all_to_all(sent, "box", split_axis=0, concat_axis=0, tiled=True)
        received = received.reshape(tiles, device_count // tiles, rhs, rank, piece)
        received = received.transpose(0, 2, 3, 1, 4).reshape(tiles, rhs, rank, LANES)
        return run_whole(received, tables, picks, order)

    near, far = pack(me, coeffs, EARLY)
    tables, picks = fetch(me, tables, pattern, tiles)
    planes = len(far)
    far = [across(far[s], s * NEAR) for s in mixed(planes)]
    near = [across(near[d], d) for d in in_turn(NEAR)]
    columns = [[z * NEAR + d for z in range(planes)] for d in range(NEAR)]
    late = lax.all_to_all(late_blocks(near), "box", 0, 0, tiled=True, axis_index_groups=columns)
    early = early_blocks(far)
    early = [across(early[d], d) for d in in_turn(NEAR)]
    done = run_first(me, tables, picks, order, early)
    return run_last(me, tables, picks, order, done, late)


def solution(mesh):
    return jax.shard_map(
        body,
        mesh=mesh,
        in_specs=(P(None, None, ("groups", "box")), P(), P(None, "groups"), P(("groups", "box"))),
        out_specs=P(None, None, ("groups", "box")),
        check_vma=False,
    )
```
